256 devices in a mesh: user: 4 (over z_lo, core), hist: 16 (over y, z_hi), fsdp: 4 (over x).
Axes of the slice: x: 4, y: 4, z: 8 (z_hi: 4, z_lo: 2; z = z_hi * 2 + z_lo), core: 2. Of those that a mesh axis runs over, the one named last changes fastest.
Arguments:
- candidates: bfloat16 [8, 4096, 1024], P('user', ('hist', 'fsdp')), parts along dimension 0, may hold values from -6 to 6
- hist_keys: bfloat16 [8, 16384, 1024], P('user', 'hist'), parts along dimension 0, may hold values from -6 to 6
- hist_values: bfloat16 [8, 16384, 1024], P('user', 'hist'), parts along dimension 0, may hold values from -6 to 6
- lengths: int32 [8], P('user'), parts along dimension 0, may hold values from 2048 to 16384, as said below
- proj_weight: bfloat16 [1024, 4096], P(('hist', 'fsdp')), may hold values from -0.1875 to 0.1875
- out_weight: bfloat16 [1024, 1024], P(('hist', 'fsdp')), may hold values from -0.1875 to 0.1875
Outputs:
- scored: bfloat16 [8, 4096, 1024], P('user', ('hist', 'fsdp')), parts along dimension 0
The draws below stay inside these ranges and needn't reach their ends.
There are 4 independent parts, one for each index of `user`. The reference program is written for one: setup_inputs(seed, part) draws one part's arguments, and reference() takes and returns one part's arrays. A program takes and returns all parts, laid end to end along the dimension named above; an argument that names none is the same for every part. Nothing has to cross between parts.
Inputs may be any that keep to these rules, and one draw needn't show every extreme that they name: `lengths`: in every group one user's history fills all 16384 slots.
All inputs are finite; a program needn't handle non-finite values.
Results may differ from the reference program's by a relative error of at most 0.014.
Values may be sent and summed in bfloat16 or wider, within the bound.
No kernel may reach another device: no remote copies, remote signals or barrier semaphores. Data moves between devices by JAX's collectives and lax.ppermute only.
A program may use at most 128 MiB of HBM per device.

```python
import jax
import jax.numpy as jnp
from jax import lax

D = 1024
HEADS = 8
HEAD_DIM = 128
USERS = 2
HISTORY = 16384
CANDS = 4096


def draw_lengths(key, part):
    key = jax.random.fold_in(key, 11)
    first, second = jax.random.split(key)
    full_user = jax.random.randint(first, (), 0, USERS)
    others = jax.random.randint(second, (USERS,), HISTORY // 8, HISTORY + 1)
    return jnp.where(jnp.arange(USERS) == full_user, HISTORY, others).astype(jnp.int32)


def level_of(stream_key, shape, pieces, smallest, top_value):
    gain, own = 1.0, jax.random.fold_in(stream_key, 6)
    for position, blocks in pieces:
        steps = jnp.exp(jax.random.uniform(jax.random.fold_in(own, position), (blocks,), jnp.float32, smallest / len(pieces), top_value / len(pieces)))
        gain = gain * jnp.repeat(steps, shape[position] // blocks).reshape([-1 if axis == position else 1 for axis in range(len(shape))])
    return gain


def normal_values(own_key, extent, spread, limit, cuts=(), kind=jnp.bfloat16):
    loudness = level_of(own_key, extent, cuts, -0.22, 0.18) if cuts else 1.0
    drawn = jax.random.normal(own_key, extent, jnp.float32) * spread * loudness
    return jnp.minimum(jnp.maximum(drawn, -limit), limit).astype(kind)


def setup_inputs(seed: int = 0, part: int = 0) -> dict:
    splits = jax.random.split(jax.random.key(seed), 7)
    part_splits = jax.random.split(jax.random.fold_in(splits[6], part), 7)
    return {
        "candidates": normal_values(part_splits[0], (USERS, CANDS, D), 1.0, 6.0, ((1, 64),)),
        "hist_keys": normal_values(part_splits[1], (USERS, HISTORY, D), 1.0, 6.0, ((1, 16),)),
        "hist_values": normal_values(part_splits[2], (USERS, HISTORY, D), 1.0, 6.0, ((1, 16),)),
        "lengths": draw_lengths(jax.random.fold_in(jax.random.fold_in(splits[6], part), 71), part),
        "proj_weight": normal_values(splits[4], (D, 4 * D), D ** -0.5, 0.1875, ((0, 64),)),
        "out_weight": normal_values(splits[5], (D, D), D ** -0.5, 0.1875, ((0, 64),)),
    }


def layer_norm(x):
    mean = lax.optimization_barrier(jnp.mean(x, axis=-1, keepdims=True))
    centered = x - mean
    var = lax.optimization_barrier(jnp.mean(centered * centered, axis=-1, keepdims=True))
    return centered * lax.rsqrt(var + 1e-06)

def reference(candidates, hist_keys, hist_values, lengths, proj_weight, out_weight):
    users = candidates.shape[0]
    scale = 1.0 / HEAD_DIM ** 0.5
    x = candidates.astype(jnp.float32)
    normed = layer_norm(x).astype(jnp.bfloat16).reshape(users * CANDS, D)
    proj = jax.nn.silu(jnp.dot(normed, proj_weight, preferred_element_type=jnp.float32))
    proj = proj.reshape(users, CANDS, 4 * D)
    gate = proj[..., :D].astype(jnp.bfloat16)
    value = proj[..., D:2 * D].astype(jnp.bfloat16)
    query = proj[..., 2 * D:3 * D].astype(jnp.bfloat16)
    key = proj[..., 3 * D:].astype(jnp.bfloat16)
    qf = query.astype(jnp.float32).reshape(users, CANDS, HEADS, HEAD_DIM)
    kf = key.astype(jnp.float32).reshape(users, CANDS, HEADS, HEAD_DIM)
    vf = value.astype(jnp.float32).reshape(users, CANDS, HEADS, HEAD_DIM)
    own_weight = jax.nn.silu(lax.optimization_barrier(jnp.sum(qf * kf, axis=-1)) * scale)
    own = (own_weight[..., None] * vf).reshape(users, CANDS, D)
    positions = jnp.arange(HISTORY, dtype=jnp.int32)
    parts = []
    for user in range(users):
        valid = positions < lengths[user]
        heads_out = []
        for head in range(HEADS):
            lo = head * HEAD_DIM
            qh = query[user, :, lo:lo + HEAD_DIM].astype(jnp.float32)
            kh = hist_keys[user, :, lo:lo + HEAD_DIM].astype(jnp.float32)
            vh = hist_values[user, :, lo:lo + HEAD_DIM].astype(jnp.float32)
            scores = jnp.dot(qh, kh.T) * scale
            weights = jnp.where(valid[None, :], jax.nn.silu(scores), 0.0).astype(jnp.bfloat16)
            heads_out.append(jnp.dot(weights.astype(jnp.float32), vh))
        parts.append(jnp.concatenate(heads_out, axis=-1))
    history_part = jnp.stack(parts)
    total = history_part + own
    mixed = (layer_norm(total) * gate.astype(jnp.float32)).astype(jnp.bfloat16)
    out = jnp.dot(mixed.reshape(users * CANDS, D), out_weight, preferred_element_type=jnp.float32)
    return (x + out.reshape(users, CANDS, D)).astype(jnp.bfloat16)
```

```python
import functools

import jax
import jax.numpy as jnp
from jax import lax
from jax.experimental import pallas as pl
from jax.experimental.pallas import tpu as pltpu
from jax.sharding import PartitionSpec as P

HEADS = 8


def layer_norm(x):
    mean = jnp.mean(x, axis=-1, keepdims=True)
    centered = x - mean
    var = jnp.mean(centered * centered, axis=-1, keepdims=True)
    return centered * lax.rsqrt(var + 1e-06)


def attend_kernel(counts, q_ref, kv_ref, o_ref, v_ref, *, spans, span, step):
    @pl.when(pl.program_id(0) == 0)
    def _():
        for s in range(spans):
            slot = lax.broadcasted_iota(jnp.int32, (span, v_ref.shape[1]), 0)
            vals = kv_ref[s, 1].astype(jnp.float32)
            v_ref[pl.ds(s * span, span), :] = jnp.where(slot < counts[s], vals, 0.0).astype(
                jnp.bfloat16
            )

    q = q_ref[...]
    total = None
    for s in range(spans):
        for j in range(0, span, step):
            keys = kv_ref[s, 0, pl.ds(j, step), :]
            half = lax.dot_general(
                q, keys, (((1,), (1,)), ((), ())), preferred_element_type=jnp.float32
            )
            weights = (half + half * jnp.tanh(half)).astype(jnp.bfloat16)
            term = jnp.dot(
                weights,
                v_ref[pl.ds(s * span + j, step), :],
                preferred_element_type=jnp.float32,
            )
            total = term if total is None else total + term
    o_ref[...] = total.astype(o_ref.dtype)


def attend(half_queries, kv, counts, block=1024, step=256):
    rows, head_dim = half_queries.shape
    spans, _, span, _ = kv.shape
    return pl.pallas_call(
        functools.partial(attend_kernel, spans=spans, span=span, step=step),
        grid_spec=pltpu.PrefetchScalarGridSpec(
            num_scalar_prefetch=1,
            grid=(rows // block,),
            in_specs=[
                pl.BlockSpec((block, head_dim), lambda i, c: (i, 0)),
                pl.BlockSpec((spans, 2, span, head_dim), lambda i, c: (0, 0, 0, 0)),
            ],
            out_specs=pl.BlockSpec((block, head_dim), lambda i, c: (i, 0)),
            scratch_shapes=[pltpu.VMEM((spans * span, head_dim), jnp.bfloat16)],
        ),
        out_shape=jax.ShapeDtypeStruct((rows, head_dim), jnp.bfloat16),
        compiler_params=pltpu.CompilerParams(vmem_limit_bytes=48 * 1024 * 1024),
        cost_estimate=pl.CostEstimate(
            flops=8 * rows * spans * span * head_dim,
            bytes_accessed=4 * rows * head_dim + 4 * spans * span * head_dim,
            transcendentals=rows * spans * span,
        ),
        name="attend",
    )(counts, half_queries, kv)


def local(sizes, candidates, hist_keys, hist_values, lengths, proj_weight, out_weight):
    hist, fsdp = sizes
    users, cand, width = candidates.shape
    head_dim = width // HEADS
    span = hist_keys.shape[1]
    both = ("hist", "fsdp")
    cols = width // fsdp
    pair = cols // head_dim
    members = users * pair
    outer = hist // members
    along_y = [[y * outer + z for y in range(members)] for z in range(outer)]
    f = lax.axis_index("fsdp")
    h = lax.axis_index("hist")
    depth = proj_weight.shape[0]

    def own_columns(cache):
        mine = lax.dynamic_slice_in_dim(cache, f * cols, cols, axis=2)
        return mine.reshape(users, span, pair, head_dim).transpose(0, 2, 1, 3)

    kv = jnp.stack([own_columns(hist_keys), own_columns(hist_values)], axis=2)
    kv = kv.reshape(members, 2, span, head_dim)
    kv = lax.all_to_all(kv, "hist", 0, 0, axis_index_groups=along_y)

    blocks = proj_weight.reshape(depth, 4, fsdp, cols).transpose(2, 0, 1, 3)

    def gather_columns(piece):
        sent = jnp.broadcast_to(piece[None], (hist,) + piece.shape)
        sent = sent.reshape((hist * fsdp,) + piece.shape[1:])
        got = lax.all_to_all(sent, both, 0, 0)
        return got.reshape(hist * fsdp * depth, -1)

    w_query = gather_columns(blocks[:, :, 2])
    w_rest = gather_columns(
        jnp.concatenate([blocks[:, :, 0], blocks[:, :, 1], blocks[:, :, 3]], axis=-1)
    )
    w_out = lax.all_gather(out_weight, both, axis=0, tiled=True)

    x = candidates.astype(jnp.float32)
    normed = layer_norm(x).astype(jnp.bfloat16)
    normed = lax.all_to_all(
        jnp.broadcast_to(normed[None], (fsdp,) + normed.shape), "fsdp", 0, 0
    )
    rows = normed.reshape(fsdp * users * cand, width)

    query = jax.nn.silu(jnp.dot(rows, w_query, preferred_element_type=jnp.float32))
    half = (query * (0.5 / head_dim**0.5)).astype(jnp.bfloat16)
    half = half.reshape(fsdp, users, cand, pair, head_dim)
    sent = half.transpose(1, 3, 0, 2, 4).reshape(members, 1, fsdp * cand, head_dim)
    sent = jnp.broadcast_to(sent, (members, outer, fsdp * cand, head_dim))
    queries = lax.all_to_all(sent.reshape(hist, fsdp * cand, head_dim), "hist", 0, 0)

    user = h // outer // pair
    starts = (jnp.arange(members, dtype=jnp.int32) * outer + h % outer) * span
    counts = jnp.clip(lengths[user] - starts, 0, span).astype(jnp.int32)
    part = attend(queries.reshape(hist * fsdp * cand, head_dim), kv, counts)
    part = lax.all_to_all(part.reshape(hist * fsdp, cand, head_dim), both, 0, 0)

    rest = jax.nn.silu(jnp.dot(rows, w_rest, preferred_element_type=jnp.float32))
    rest = rest.astype(jnp.bfloat16).reshape(fsdp, users, cand, 3, pair, head_dim)
    gate, value, key = rest[..., 0, :, :], rest[..., 1, :, :], rest[..., 2, :, :]
    score = 2.0 * jnp.sum(
        half.astype(jnp.float32) * key.astype(jnp.float32), axis=-1, keepdims=True
    )
    own = (jax.nn.silu(score) * value.astype(jnp.float32)).astype(jnp.bfloat16)
    back = jnp.stack([own, gate], axis=3).reshape(fsdp, users, cand, 2, cols)
    back = lax.all_to_all(back, "fsdp", 0, 0)
    back = back.transpose(3, 1, 2, 0, 4).reshape(2, users, cand, width)

    part = part.reshape(users, pair, outer, fsdp, cand, head_dim).astype(jnp.float32)
    total = jnp.sum(part, axis=2).transpose(0, 3, 2, 1, 4).reshape(users, cand, width)
    total = total + back[0].astype(jnp.float32)
    mixed = (layer_norm(total) * back[1].astype(jnp.float32)).astype(jnp.bfloat16)
    projected = jnp.dot(
        mixed.reshape(users * cand, width), w_out, preferred_element_type=jnp.float32
    )
    return (x + projected.reshape(users, cand, width)).astype(jnp.bfloat16)


def solution(mesh):
    placed = (
        P("user", ("hist", "fsdp"), None),
        P("user", "hist", None),
        P("user", "hist", None),
        P("user"),
        P(("hist", "fsdp"), None),
        P(("hist", "fsdp"), None),
    )
    sizes = (mesh.shape["hist"], mesh.shape["fsdp"])
    return jax.shard_map(
        functools.partial(local, sizes),
        mesh=mesh,
        in_specs=placed,
        out_specs=P("user", ("hist", "fsdp"), None),
        check_vma=False,
    )
```

```python
import functools

import jax
import jax.numpy as jnp
from jax import lax
from jax.experimental import pallas as pl
from jax.experimental.pallas import tpu as pltpu
from jax.sharding import PartitionSpec as P

HEADS = 8


IN_VMEM = pl.BlockSpec(memory_space=pltpu.VMEM)
IN_SMEM = pl.BlockSpec(memory_space=pltpu.SMEM)


def layer_norm(x):
    mean = jnp.mean(x, axis=-1, keepdims=True)
    centered = x - mean
    var = jnp.mean(centered * centered, axis=-1, keepdims=True)
    return centered * lax.rsqrt(var + 1e-06)


def small_call(kernel, name, out_shape, *args, scalars=0, scratch=(), flops=0):
    specs = [IN_SMEM] * scalars + [IN_VMEM] * (len(args) - scalars)
    return pl.pallas_call(
        kernel,
        in_specs=specs,
        out_specs=jax.tree.map(lambda _: IN_VMEM, out_shape),
        out_shape=out_shape,
        scratch_shapes=scratch,
        compiler_params=pltpu.CompilerParams(vmem_limit_bytes=32 * 1024 * 1024),
        cost_estimate=pl.CostEstimate(flops=flops, bytes_accessed=1 << 20, transcendentals=0),
        name=name,
    )(*args)


def normalise_kernel(x_ref, o_ref):
    for u in range(x_ref.shape[0]):
        o_ref[u] = layer_norm(x_ref[u].astype(jnp.float32)).astype(o_ref.dtype)


def query_kernel(place, *refs, scale):
    *rows, w_ref, o_ref = refs
    fsdp = len(rows)
    members, _, cand, head_dim = o_ref.shape
    pair = members // rows[0].shape[0]
    w = w_ref[:, : pair * head_dim]
    for m, row in enumerate(rows):
        at = lax.rem(place[0] + m, fsdp)
        for u in range(row.shape[0]):
            out = jax.nn.silu(jnp.dot(row[u], w, preferred_element_type=jnp.float32))
            out = (out * scale).astype(jnp.bfloat16)
            for e in range(pair):
                o_ref[u * pair + e, at] = out[:, e * head_dim : (e + 1) * head_dim]


def rest_kernel(place, *refs):
    fsdp = (len(refs) - 3) // 2
    rows, (q_ref, mine, other), outs = refs[:fsdp], refs[fsdp : fsdp + 3], refs[fsdp + 3 :]
    members, _, cand, head_dim = q_ref.shape
    users = rows[0].shape[0]
    pair = members // users
    first = pair * head_dim
    for turn, w_ref in enumerate((mine, other)):
        head = lax.rem(place[1] + turn, 2)
        here = pl.ds(pl.multiple_of(head * head_dim, head_dim), head_dim)
        w = w_ref[:, first : first + 3 * head_dim]
        for m in range(fsdp):
            at = lax.rem(place[0] + m, fsdp)
            for u in range(users):
                out = jax.nn.silu(jnp.dot(rows[m][u], w, preferred_element_type=jnp.float32))
                out = out.astype(jnp.bfloat16)
                gate = out[:, :head_dim]
                value = out[:, head_dim : 2 * head_dim].astype(jnp.float32)
                key = out[:, 2 * head_dim :].astype(jnp.float32)
                half = q_ref[u * pair + head, at].astype(jnp.float32)
                score = 2.0 * jnp.sum(half * key, axis=-1, keepdims=True)
                outs[m][0, u, :, here] = (jax.nn.silu(score) * value).astype(jnp.bfloat16)
                outs[m][1, u, :, here] = gate


def finish_kernel(place, x_ref, t_ref, *refs):
    *backs, mine, other, o_ref, total, gate = refs
    fsdp = len(backs)
    users, cand, width = x_ref.shape
    pair = t_ref.shape[0] // users // fsdp
    head_dim = t_ref.shape[-1]
    cols = width // fsdp
    for u in range(users):
        for e in range(pair):
            for c in range(fsdp):
                lo = c * cols + e * head_dim
                total[u, :, lo : lo + head_dim] = t_ref[(u * pair + e) * fsdp + c].astype(
                    jnp.float32
                )
    for m, back in enumerate(backs):
        lo = pl.multiple_of(lax.rem(place[0] + fsdp - m, fsdp) * cols, cols)
        for u in range(users):
            total[u, :, pl.ds(lo, cols)] += back[0, u].astype(jnp.float32)
            gate[u, :, pl.ds(lo, cols)] = back[1, u].astype(jnp.float32)
    half = width // 2
    for u in range(users):
        mixed = (layer_norm(total[u]) * gate[u]).astype(jnp.bfloat16)
        for turn, w_ref in enumerate((mine, other)):
            lo = pl.multiple_of(lax.rem(place[1] + turn, 2) * half, half)
            w = w_ref[:, w_ref.shape[1] - half :]
            out = jnp.dot(mixed, w, preferred_element_type=jnp.float32)
            out += x_ref[u, :, pl.ds(lo, half)].astype(jnp.float32)
            o_ref[u, :, pl.ds(lo, half)] = out.astype(o_ref.dtype)


def attend_kernel(counts, q_ref, *refs, step):
    *caches, o_ref, v_ref = refs
    span = caches[0].shape[1]

    slot = lax.broadcasted_iota(jnp.int32, (span, v_ref.shape[1]), 0)
    for s, cache in enumerate(caches):
        vals = jnp.where(slot < counts[s], cache[1].astype(jnp.float32), 0.0)
        v_ref[pl.ds(s * span, span), :] = vals.astype(jnp.bfloat16)

    q = q_ref[...]
    total = None
    for s, cache in enumerate(caches):
        for j in range(0, span, step):
            half = lax.dot_general(
                q,
                cache[0, pl.ds(j, step), :],
                (((1,), (1,)), ((), ())),
                preferred_element_type=jnp.float32,
            )
            weights = (half + half * jnp.tanh(half)).astype(jnp.bfloat16)
            term = jnp.dot(
                weights,
                v_ref[pl.ds(s * span + j, step), :],
                preferred_element_type=jnp.float32,
            )
            total = term if total is None else total + term
    o_ref[...] = total.astype(o_ref.dtype)


def attend(half_queries, caches, counts, step=256):
    rows, head_dim = half_queries.shape
    _, span, _ = caches[0].shape
    slots = len(caches) * span
    in_vmem = pl.BlockSpec(memory_space=pltpu.VMEM)
    return pl.pallas_call(
        functools.partial(attend_kernel, step=step),
        in_specs=[pl.BlockSpec(memory_space=pltpu.SMEM)] + [in_vmem] * (1 + len(caches)),
        out_specs=in_vmem,
        scratch_shapes=[pltpu.VMEM((slots, head_dim), jnp.bfloat16)],
        out_shape=jax.ShapeDtypeStruct((rows, head_dim), jnp.bfloat16),
        compiler_params=pltpu.CompilerParams(vmem_limit_bytes=32 * 1024 * 1024),
        cost_estimate=pl.CostEstimate(
            flops=8 * rows * slots * head_dim,
            bytes_accessed=4 * rows * head_dim + 4 * slots * head_dim,
            transcendentals=rows * slots,
        ),
        name="attend",
    )(counts, half_queries, *caches)


def local(sizes, candidates, hist_keys, hist_values, lengths, proj_weight, out_weight):
    user_axis, hist, fsdp = sizes
    users, cand, width = candidates.shape
    head_dim = width // HEADS
    span = hist_keys.shape[1]
    both = ("hist", "fsdp")
    cols = width // fsdp
    pair = cols // head_dim
    members = users * pair
    outer = hist // members
    f = lax.axis_index("fsdp")
    h = lax.axis_index("hist")
    y, z = lax.div(h, outer), lax.rem(h, outer)
    core = lax.rem(lax.axis_index("user"), 2)
    depth = proj_weight.shape[0]
    along_y = [[a * outer + b for a in range(members)] for b in range(outer)]
    across = [
        [(a * outer + b) * fsdp + c for a in range(members) for c in range(fsdp)]
        for b in range(outer)
    ]

    def shift_x(a, k):
        return lax.ppermute(a, "fsdp", [(i, (i + k) % fsdp) for i in range(fsdp)])

    def shift_y(a, k):
        to = [(i, (i + k * outer) % hist) for i in range(hist)]
        return lax.ppermute(a, "hist", to)

    def shift_z(a, k):
        to = [(i, i - i % outer + (i + k) % outer) for i in range(hist)]
        return lax.ppermute(a, "hist", to)

    def swap_core(a):
        return lax.ppermute(a, "user", [(i, i ^ 1) for i in range(user_axis)])

    place = jnp.stack([f, core]).astype(jnp.int32)

    def like(*shape):
        return jax.ShapeDtypeStruct(shape, jnp.bfloat16)

    normed = small_call(
        normalise_kernel, "normalise", like(*candidates.shape), candidates, flops=1 << 20
    )
    rows = [normed] + [shift_x(normed, -m) for m in range(1, fsdp)]

    blocks = proj_weight.reshape(depth, 4, fsdp, pair, head_dim).transpose(2, 0, 1, 3, 4)
    mine = lax.dynamic_index_in_dim(blocks, core, axis=3, keepdims=False)
    part_out = lax.dynamic_slice_in_dim(out_weight, core * (width // 2), width // 2, axis=1)
    part_out = jnp.broadcast_to(part_out[None], (fsdp, depth, width // 2))
    sent = jnp.concatenate(
        [blocks[:, :, 2].reshape(fsdp, depth, cols)]
        + [mine[:, :, 0], mine[:, :, 1], mine[:, :, 3], part_out],
        axis=-1,
    )
    sent = jnp.broadcast_to(sent[None], (hist,) + sent.shape).reshape(hist * fsdp, depth, -1)
    weights = lax.all_to_all(sent, both, 0, 0).reshape(width, -1)
    def own_cache(member):
        at = (lax.div(member, pair), 0, f * cols + lax.rem(member, pair) * head_dim)
        size = (1, span, head_dim)
        return jnp.concatenate(
            [lax.dynamic_slice(hist_keys, at, size), lax.dynamic_slice(hist_values, at, size)]
        )

    caches = [own_cache(y)]
    caches += [shift_y(own_cache(lax.rem(y + k, members)), k) for k in range(1, members)]
    weights, caches, rows = lax.optimization_barrier((weights, caches, rows))
    w_other = swap_core(weights)

    work = 2 * fsdp * users * cand * width
    half = small_call(
        functools.partial(query_kernel, scale=0.5 / head_dim**0.5),
        "query",
        like(members, fsdp, cand, head_dim),
        place,
        *rows,
        weights,
        scalars=1,
        flops=work * cols,
    )
    sent = half.reshape(members, fsdp * cand, head_dim)
    queries = lax.all_to_all(sent, "hist", 0, 0, axis_index_groups=along_y)
    queries = queries.reshape(members * fsdp * cand, head_dim)

    queries = [queries] + [shift_z(queries, -m) for m in range(1, outer)]

    sources = lax.rem(y + members - jnp.arange(members, dtype=jnp.int32), members)
    starts = (sources * outer + z) * span
    counts = jnp.clip(lengths[lax.div(y, pair)] - starts, 0, span).astype(jnp.int32)
    back = small_call(
        rest_kernel,
        "rest",
        [like(2, users, cand, cols)] * fsdp,
        place,
        *rows,
        half,
        weights,
        w_other,
        scalars=1,
        flops=work * cols * 3,
    )
    split = queries[0].shape[0] // 2
    head, tail = queries[0][:split], queries[0][split:]
    own = [attend(head, caches, counts)]
    last = (own[0], back)
    parts = []
    for m in [1, outer - 1] + list(range(2, outer - 1)):
        ready, last = lax.optimization_barrier((queries[m], last))
        if not parts:
            own[0], back = last
            back = [back[0]] + [shift_x(back[k], k) for k in range(1, fsdp)]
        last = attend(ready, caches, counts)
        parts.append(shift_z(last, m))
    tail, last = lax.optimization_barrier((tail, last))
    own.append(attend(tail, caches, counts))
    parts.append(jnp.concatenate(own))

    total = sum(p.astype(jnp.float32) for p in parts).astype(jnp.bfloat16)
    total, back = lax.optimization_barrier((total, back))
    total = total.reshape(members * fsdp, cand, head_dim)
    total = lax.all_to_all(total, both, 0, 0, axis_index_groups=across)
    wide = pltpu.VMEM((users, cand, width), jnp.float32)
    return small_call(
        finish_kernel,
        "finish",
        like(users, cand, width),
        place,
        candidates,
        total,
        *back,
        weights,
        w_other,
        scalars=1,
        scratch=[wide, wide],
        flops=2 * users * cand * width * width,
    )


def solution(mesh):
    placed = (
        P("user", ("hist", "fsdp"), None),
        P("user", "hist", None),
        P("user", "hist", None),
        P("user"),
        P(("hist", "fsdp"), None),
        P(("hist", "fsdp"), None),
    )
    sizes = (mesh.shape["user"], mesh.shape["hist"], mesh.shape["fsdp"])
    return jax.shard_map(
        functools.partial(local, sizes),
        mesh=mesh,
        in_specs=placed,
        out_specs=P("user", ("hist", "fsdp"), None),
        check_vma=False,
    )
```

```python
import functools

import jax
import jax.numpy as jnp
from jax import lax
from jax.experimental import pallas as pl
from jax.experimental.pallas import tpu as pltpu
from jax.sharding import PartitionSpec as P

HEADS = 8


IN_SMEM = pl.BlockSpec(memory_space=pltpu.SMEM)


def layer_norm(x):
    mean = jnp.mean(x, axis=-1, keepdims=True)
    centered = x - mean
    var = jnp.mean(centered * centered, axis=-1, keepdims=True)
    return centered * lax.rsqrt(var + 1e-06)


def small_call(kernel, name, out_shape, *args, scalars=0, scratch=(), blocks=None, flops=0):
    specs = [IN_SMEM] * scalars
    for n, a in enumerate(args[scalars:]):
        width, at = (blocks or {}).get(n + scalars - len(args), (a.shape[-1], 0))
        zeros = (0,) * (a.ndim - 1)
        specs.append(pl.BlockSpec(a.shape[:-1] + (width,), lambda i, z=zeros, c=at: z + (c,)))
    return pl.pallas_call(
        kernel,
        grid=(1,),
        in_specs=specs,
        out_specs=jax.tree.map(
            lambda o: pl.BlockSpec(o.shape, lambda i, n=len(o.shape): (0,) * n), out_shape
        ),
        out_shape=out_shape,
        scratch_shapes=scratch,
        compiler_params=pltpu.CompilerParams(vmem_limit_bytes=60 * 1024 * 1024),
        cost_estimate=pl.CostEstimate(flops=flops, bytes_accessed=1 << 20, transcendentals=0),
        name=name,
    )(*args)


def normalise_kernel(x_ref, o_ref):
    for u in range(x_ref.shape[0]):
        o_ref[u] = layer_norm(x_ref[u].astype(jnp.float32)).astype(o_ref.dtype)


def query_kernel(place, *refs, scale):
    *rows, w_ref, o_ref = refs
    fsdp = len(rows)
    members, _, cand, head_dim = o_ref.shape
    pair = members // rows[0].shape[0]
    w = w_ref[...]
    for m, row in enumerate(rows):
        at = lax.rem(place[0] + m, fsdp)
        for u in range(row.shape[0]):
            out = jax.nn.silu(jnp.dot(row[u], w, preferred_element_type=jnp.float32))
            out = (out * scale).astype(jnp.bfloat16)
            for e in range(pair):
                o_ref[u * pair + e, at] = out[:, e * head_dim : (e + 1) * head_dim]


def rest_kernel(place, *refs):
    fsdp = (len(refs) - 3) // 2
    rows, (q_ref, mine, other), outs = refs[:fsdp], refs[fsdp : fsdp + 3], refs[fsdp + 3 :]
    members, _, cand, head_dim = q_ref.shape
    users = rows[0].shape[0]
    pair = members // users
    for turn, w_ref in enumerate((mine, other)):
        head = lax.rem(place[1] + turn, 2)
        here = pl.ds(pl.multiple_of(head * head_dim, head_dim), head_dim)
        w = w_ref[...]
        for m in range(fsdp):
            at = lax.rem(place[0] + m, fsdp)
            for u in range(users):
                out = jax.nn.silu(jnp.dot(rows[m][u], w, preferred_element_type=jnp.float32))
                out = out.astype(jnp.bfloat16)
                gate = out[:, :head_dim]
                value = out[:, head_dim : 2 * head_dim].astype(jnp.float32)
                key = out[:, 2 * head_dim :].astype(jnp.float32)
                half = q_ref[u * pair + head, at].astype(jnp.float32)
                score = 2.0 * jnp.sum(half * key, axis=-1, keepdims=True)
                outs[m][0, u, :, here] = (jax.nn.silu(score) * value).astype(jnp.bfloat16)
                outs[m][1, u, :, here] = gate


def finish_kernel(place, x_ref, t_ref, *refs):
    fsdp = (len(refs) - 3) // 2
    backs, weights, (o_ref, total, gate) = refs[:fsdp], refs[fsdp:-3], refs[-3:]
    users, cand, width = x_ref.shape
    pair = t_ref.shape[0] // users // fsdp
    head_dim = t_ref.shape[-1]
    cols = width // fsdp
    for u in range(users):
        for e in range(pair):
            for c in range(fsdp):
                lo = c * cols + e * head_dim
                total[u, :, lo : lo + head_dim] = t_ref[(u * pair + e) * fsdp + c].astype(
                    jnp.float32
                )
    for m, back in enumerate(backs):
        lo = pl.multiple_of(lax.rem(place[0] + fsdp - m, fsdp) * cols, cols)
        for u in range(users):
            total[u, :, pl.ds(lo, cols)] += back[0, u].astype(jnp.float32)
            gate[u, :, pl.ds(lo, cols)] = back[1, u].astype(jnp.float32)
    part = cols // 2
    for u in range(users):
        mixed = (layer_norm(total[u]) * gate[u]).astype(jnp.bfloat16)
        for m, w_ref in enumerate(weights):
            out = jnp.dot(mixed, w_ref[...], preferred_element_type=jnp.float32)
            for turn in range(2):
                lo = lax.rem(place[0] + fsdp - m, fsdp) * cols
                lo = pl.multiple_of(lo + lax.rem(place[1] + turn, 2) * part, part)
                here = out[:, turn * part : (turn + 1) * part]
                here += x_ref[u, :, pl.ds(lo, part)].astype(jnp.float32)
                o_ref[u, :, pl.ds(lo, part)] = here.astype(o_ref.dtype)


def attend_kernel(counts, q_ref, *refs, step):
    *caches, o_ref, v_ref = refs
    span = caches[0].shape[1]

    slot = lax.broadcasted_iota(jnp.int32, (span, v_ref.shape[1]), 0)
    for s, cache in enumerate(caches):
        vals = jnp.where(slot < counts[s], cache[1].astype(jnp.float32), 0.0)
        v_ref[pl.ds(s * span, span), :] = vals.astype(jnp.bfloat16)

    q = q_ref[...]
    total = None
    for s, cache in enumerate(caches):
        for j in range(0, span, step):
            half = lax.dot_general(
                q,
                cache[0, pl.ds(j, step), :],
                (((1,), (1,)), ((), ())),
                preferred_element_type=jnp.float32,
            )
            weights = (half + half * jnp.tanh(half)).astype(jnp.bfloat16)
            term = jnp.dot(
                weights,
                v_ref[pl.ds(s * span + j, step), :],
                preferred_element_type=jnp.float32,
            )
            total = term if total is None else total + term
    o_ref[...] = total.astype(o_ref.dtype)


def attend(half_queries, caches, counts, step=256):
    rows, head_dim = half_queries.shape
    _, span, _ = caches[0].shape
    slots = len(caches) * span
    in_vmem = pl.BlockSpec(memory_space=pltpu.VMEM)
    return pl.pallas_call(
        functools.partial(attend_kernel, step=step),
        in_specs=[pl.BlockSpec(memory_space=pltpu.SMEM)] + [in_vmem] * (1 + len(caches)),
        out_specs=in_vmem,
        scratch_shapes=[pltpu.VMEM((slots, head_dim), jnp.bfloat16)],
        out_shape=jax.ShapeDtypeStruct((rows, head_dim), jnp.bfloat16),
        compiler_params=pltpu.CompilerParams(vmem_limit_bytes=32 * 1024 * 1024),
        cost_estimate=pl.CostEstimate(
            flops=8 * rows * slots * head_dim,
            bytes_accessed=4 * rows * head_dim + 4 * slots * head_dim,
            transcendentals=rows * slots,
        ),
        name="attend",
    )(counts, half_queries, *caches)


def local(sizes, candidates, hist_keys, hist_values, lengths, proj_weight, out_weight):
    user_axis, hist, fsdp = sizes
    users, cand, width = candidates.shape
    head_dim = width // HEADS
    span = hist_keys.shape[1]
    both = ("hist", "fsdp")
    cols = width // fsdp
    pair = cols // head_dim
    members = users * pair
    outer = hist // members
    f = lax.axis_index("fsdp")
    h = lax.axis_index("hist")
    y, z = lax.div(h, outer), lax.rem(h, outer)
    core = lax.rem(lax.axis_index("user"), 2)
    depth = proj_weight.shape[0]
    along_y = [[a * outer + b for a in range(members)] for b in range(outer)]
    across = [
        [(a * outer + b) * fsdp + c for a in range(members) for c in range(fsdp)]
        for b in range(outer)
    ]

    def shift_x(a, k):
        return lax.ppermute(a, "fsdp", [(i, (i + k) % fsdp) for i in range(fsdp)])

    def shift_y(a, k):
        to = [(i, (i + k * outer) % hist) for i in range(hist)]
        return lax.ppermute(a, "hist", to)

    def shift_z(a, k):
        to = [(i, i - i % outer + (i + k) % outer) for i in range(hist)]
        return lax.ppermute(a, "hist", to)

    def swap_core(a):
        return lax.ppermute(a, "user", [(i, i ^ 1) for i in range(user_axis)])

    place = jnp.stack([f, core]).astype(jnp.int32)

    def like(*shape):
        return jax.ShapeDtypeStruct(shape, jnp.bfloat16)

    normed = small_call(
        normalise_kernel, "normalise", like(*candidates.shape), candidates, flops=1 << 20
    )
    rows = [normed] + [shift_x(normed, -m) for m in range(1, fsdp)]

    blocks = proj_weight.reshape(depth, 4, fsdp, pair, head_dim).transpose(2, 0, 1, 3, 4)
    mine = lax.dynamic_index_in_dim(blocks, core, axis=3, keepdims=False)
    eighth = out_weight.reshape(depth, fsdp, 2, cols // 2).transpose(1, 2, 0, 3)
    eighth = lax.dynamic_index_in_dim(eighth, core, axis=1, keepdims=False)
    sent = [blocks[:, :, 2].reshape(fsdp, depth, cols), eighth]
    sent = jnp.concatenate(sent + [mine[:, :, 0], mine[:, :, 1], mine[:, :, 3]], axis=-1)
    sent = jnp.broadcast_to(sent[None], (hist,) + sent.shape).reshape(hist * fsdp, depth, -1)
    weights = lax.all_to_all(sent, both, 0, 0).reshape(width, -1)
    def own_cache(member):
        at = (lax.div(member, pair), 0, f * cols + lax.rem(member, pair) * head_dim)
        size = (1, span, head_dim)
        return jnp.concatenate(
            [lax.dynamic_slice(hist_keys, at, size), lax.dynamic_slice(hist_values, at, size)]
        )

    caches = [own_cache(y)]
    caches += [shift_y(own_cache(lax.rem(y + k, members)), k) for k in range(1, members)]
    weights, caches, rows = lax.optimization_barrier((weights, caches, rows))
    w_other = swap_core(weights)

    work = 2 * fsdp * users * cand * width
    half = small_call(
        functools.partial(query_kernel, scale=0.5 / head_dim**0.5),
        "query",
        like(members, fsdp, cand, head_dim),
        place,
        *rows,
        weights,
        scalars=1,
        blocks={-1: (cols, 0)},
        flops=work * cols,
    )
    sent = half.reshape(members, fsdp * cand, head_dim)
    queries = lax.all_to_all(sent, "hist", 0, 0, axis_index_groups=along_y)
    queries = queries.reshape(members * fsdp * cand, head_dim)

    queries = [queries] + [shift_z(queries, -m) for m in range(1, outer)]

    w_out = [w[:, cols : cols + cols // 2] for w in (weights, w_other)]
    w_out = jnp.concatenate(w_out, axis=-1)
    w_out = [w_out] + [shift_x(w_out, m) for m in range(1, fsdp)]

    sources = lax.rem(y + members - jnp.arange(members, dtype=jnp.int32), members)
    starts = (sources * outer + z) * span
    counts = jnp.clip(lengths[lax.div(y, pair)] - starts, 0, span).astype(jnp.int32)
    back = small_call(
        rest_kernel,
        "rest",
        [like(2, users, cand, cols)] * fsdp,
        place,
        *rows,
        half,
        weights,
        w_other,
        scalars=1,
        blocks={-2: (3 * head_dim, 1), -1: (3 * head_dim, 1)},
        flops=work * cols * 3,
    )
    split = queries[0].shape[0] // 2
    head, tail = queries[0][:split], queries[0][split:]
    own = [attend(head, caches, counts)]
    last = own[0]
    parts = []
    for m in [1, outer - 1] + list(range(2, outer - 1)):
        ready, last = lax.optimization_barrier((queries[m], last))
        if not parts:
            own[0] = last
        last = attend(ready, caches, counts)
        parts.append(shift_z(last, m))
    tail, last, w_out = lax.optimization_barrier((tail, last, w_out))
    own.append(attend(tail, caches, counts))
    parts.append(jnp.concatenate(own))
    back = [back[0]] + [shift_x(back[k], k) for k in range(1, fsdp)]

    total = sum(p.astype(jnp.float32) for p in parts).astype(jnp.bfloat16)
    total, back = lax.optimization_barrier((total, back))
    total = total.reshape(members * fsdp, cand, head_dim)
    total = lax.all_to_all(total, both, 0, 0, axis_index_groups=across)
    wide = pltpu.VMEM((users, cand, width), jnp.float32)
    return small_call(
        finish_kernel,
        "finish",
        like(users, cand, width),
        place,
        candidates,
        total,
        *back,
        *w_out,
        scalars=1,
        scratch=[wide, wide],
        flops=2 * users * cand * width * width,
    )


def solution(mesh):
    placed = (
        P("user", ("hist", "fsdp"), None),
        P("user", "hist", None),
        P("user", "hist", None),
        P("user"),
        P(("hist", "fsdp"), None),
        P(("hist", "fsdp"), None),
    )
    sizes = (mesh.shape["user"], mesh.shape["hist"], mesh.shape["fsdp"])
    return jax.shard_map(
        functools.partial(local, sizes),
        mesh=mesh,
        in_specs=placed,
        out_specs=P("user", ("hist", "fsdp"), None),
        check_vma=False,
    )
```

```python
import functools

import jax
import jax.numpy as jnp
from jax import lax
from jax.experimental import pallas as pl
from jax.experimental.pallas import tpu as pltpu
from jax.sharding import PartitionSpec as P

HEADS = 8


IN_SMEM = pl.BlockSpec(memory_space=pltpu.SMEM)


def layer_norm(x):
    mean = jnp.mean(x, axis=-1, keepdims=True)
    centered = x - mean
    var = jnp.mean(centered * centered, axis=-1, keepdims=True)
    return centered * lax.rsqrt(var + 1e-06)


def small_call(kernel, name, out_shape, *args, scalars=0, scratch=(), blocks=None, flops=0):
    specs = [IN_SMEM] * scalars
    for n, a in enumerate(args[scalars:]):
        width, at = (blocks or {}).get(n + scalars - len(args), (a.shape[-1], 0))
        zeros = (0,) * (a.ndim - 1)
        specs.append(pl.BlockSpec(a.shape[:-1] + (width,), lambda i, z=zeros, c=at: z + (c,)))
    return pl.pallas_call(
        kernel,
        grid=(1,),
        in_specs=specs,
        out_specs=jax.tree.map(
            lambda o: pl.BlockSpec(o.shape, lambda i, n=len(o.shape): (0,) * n), out_shape
        ),
        out_shape=out_shape,
        scratch_shapes=scratch,
        compiler_params=pltpu.CompilerParams(vmem_limit_bytes=60 * 1024 * 1024),
        cost_estimate=pl.CostEstimate(flops=flops, bytes_accessed=1 << 20, transcendentals=0),
        name=name,
    )(*args)


def normalise_kernel(x_ref, o_ref):
    for u in range(x_ref.shape[0]):
        o_ref[u] = layer_norm(x_ref[u].astype(jnp.float32)).astype(o_ref.dtype)


def query_kernel(place, *refs, scale):
    *rows, w_ref, o_ref = refs
    fsdp = len(rows)
    members, _, cand, head_dim = o_ref.shape
    pair = members // rows[0].shape[0]
    w = w_ref[...]
    for m, row in enumerate(rows):
        at = lax.rem(place[0] + m, fsdp)
        for u in range(row.shape[0]):
            out = jax.nn.silu(jnp.dot(row[u], w, preferred_element_type=jnp.float32))
            out = (out * scale).astype(jnp.bfloat16)
            for e in range(pair):
                o_ref[u * pair + e, at] = out[:, e * head_dim : (e + 1) * head_dim]


def rest_kernel(place, *refs):
    fsdp = (len(refs) - 3) // 2
    rows, (q_ref, mine, other), outs = refs[:fsdp], refs[fsdp : fsdp + 3], refs[fsdp + 3 :]
    members, _, cand, head_dim = q_ref.shape
    users = rows[0].shape[0]
    pair = members // users
    for turn, w_ref in enumerate((mine, other)):
        head = lax.rem(place[1] + turn, 2)
        here = pl.ds(pl.multiple_of(head * head_dim, head_dim), head_dim)
        w = w_ref[...]
        for m in range(fsdp):
            at = lax.rem(place[0] + m, fsdp)
            for u in range(users):
                out = jax.nn.silu(jnp.dot(rows[m][u], w, preferred_element_type=jnp.float32))
                out = out.astype(jnp.bfloat16)
                gate = out[:, :head_dim]
                value = out[:, head_dim : 2 * head_dim].astype(jnp.float32)
                key = out[:, 2 * head_dim :].astype(jnp.float32)
                half = q_ref[u * pair + head, at].astype(jnp.float32)
                score = 2.0 * jnp.sum(half * key, axis=-1, keepdims=True)
                outs[m][0, u, :, here] = (jax.nn.silu(score) * value).astype(jnp.bfloat16)
                outs[m][1, u, :, here] = gate


def finish_kernel(place, x_ref, t_ref, *refs):
    fsdp = (len(refs) - 3) // 2
    backs, weights, (o_ref, total, gate) = refs[:fsdp], refs[fsdp:-3], refs[-3:]
    users, cand, width = x_ref.shape
    pair = t_ref.shape[0] // users // fsdp
    head_dim = t_ref.shape[-1]
    cols = width // fsdp
    for u in range(users):
        for e in range(pair):
            for c in range(fsdp):
                lo = c * cols + e * head_dim
                total[u, :, lo : lo + head_dim] = t_ref[(u * pair + e) * fsdp + c].astype(
                    jnp.float32
                )
    for m, back in enumerate(backs):
        lo = pl.multiple_of(lax.rem(place[0] + fsdp - m, fsdp) * cols, cols)
        for u in range(users):
            total[u, :, pl.ds(lo, cols)] += back[0, u].astype(jnp.float32)
            gate[u, :, pl.ds(lo, cols)] = back[1, u].astype(jnp.float32)
    part = cols // 2
    for u in range(users):
        mixed = (layer_norm(total[u]) * gate[u]).astype(jnp.bfloat16)
        for m, w_ref in enumerate(weights):
            out = jnp.dot(mixed, w_ref[...], preferred_element_type=jnp.float32)
            for turn in range(2):
                lo = lax.rem(place[0] + fsdp - m, fsdp) * cols
                lo = pl.multiple_of(lo + lax.rem(place[1] + turn, 2) * part, part)
                here = out[:, turn * part : (turn + 1) * part]
                here += x_ref[u, :, pl.ds(lo, part)].astype(jnp.float32)
                o_ref[u, :, pl.ds(lo, part)] = here.astype(o_ref.dtype)


def attend_kernel(counts, q_ref, *refs, step):
    *caches, o_ref, v_ref = refs
    span = caches[0].shape[1]

    slot = lax.broadcasted_iota(jnp.int32, (span, v_ref.shape[1]), 0)
    for s, cache in enumerate(caches):
        vals = jnp.where(slot < counts[s], cache[1].astype(jnp.float32), 0.0)
        v_ref[pl.ds(s * span, span), :] = vals.astype(jnp.bfloat16)

    q = q_ref[...]
    total = None
    for s, cache in enumerate(caches):
        for j in range(0, span, step):
            half = lax.dot_general(
                q,
                cache[0, pl.ds(j, step), :],
                (((1,), (1,)), ((), ())),
                preferred_element_type=jnp.float32,
            )
            weights = (half + half * jnp.tanh(half)).astype(jnp.bfloat16)
            term = jnp.dot(
                weights,
                v_ref[pl.ds(s * span + j, step), :],
                preferred_element_type=jnp.float32,
            )
            total = term if total is None else total + term
    o_ref[...] = total.astype(o_ref.dtype)


def attend(half_queries, caches, counts, step=256):
    rows, head_dim = half_queries.shape
    _, span, _ = caches[0].shape
    slots = len(caches) * span
    in_vmem = pl.BlockSpec(memory_space=pltpu.VMEM)
    return pl.pallas_call(
        functools.partial(attend_kernel, step=step),
        in_specs=[pl.BlockSpec(memory_space=pltpu.SMEM)] + [in_vmem] * (1 + len(caches)),
        out_specs=in_vmem,
        scratch_shapes=[pltpu.VMEM((slots, head_dim), jnp.bfloat16)],
        out_shape=jax.ShapeDtypeStruct((rows, head_dim), jnp.bfloat16),
        compiler_params=pltpu.CompilerParams(vmem_limit_bytes=32 * 1024 * 1024),
        cost_estimate=pl.CostEstimate(
            flops=8 * rows * slots * head_dim,
            bytes_accessed=4 * rows * head_dim + 4 * slots * head_dim,
            transcendentals=rows * slots,
        ),
        name="attend",
    )(counts, half_queries, *caches)


def local(sizes, candidates, hist_keys, hist_values, lengths, proj_weight, out_weight):
    user_axis, hist, fsdp = sizes
    users, cand, width = candidates.shape
    head_dim = width // HEADS
    span = hist_keys.shape[1]
    both = ("hist", "fsdp")
    cols = width // fsdp
    pair = cols // head_dim
    members = users * pair
    outer = hist // members
    f = lax.axis_index("fsdp")
    h = lax.axis_index("hist")
    y, z = lax.div(h, outer), lax.rem(h, outer)
    core = lax.rem(lax.axis_index("user"), 2)
    depth = proj_weight.shape[0]
    along_y = [[a * outer + b for a in range(members)] for b in range(outer)]
    across = [
        [(a * outer + b) * fsdp + c for a in range(members) for c in range(fsdp)]
        for b in range(outer)
    ]

    def shift_x(a, k):
        return lax.ppermute(a, "fsdp", [(i, (i + k) % fsdp) for i in range(fsdp)])

    def shift_y(a, k):
        to = [(i, (i + k * outer) % hist) for i in range(hist)]
        return lax.ppermute(a, "hist", to)

    def shift_z(a, k):
        to = [(i, i - i % outer + (i + k) % outer) for i in range(hist)]
        return lax.ppermute(a, "hist", to)

    def swap_core(a):
        return lax.ppermute(a, "user", [(i, i ^ 1) for i in range(user_axis)])

    place = jnp.stack([f, core]).astype(jnp.int32)

    def like(*shape):
        return jax.ShapeDtypeStruct(shape, jnp.bfloat16)

    normed = small_call(
        normalise_kernel, "normalise", like(*candidates.shape), candidates, flops=1 << 20
    )
    rows = [normed] + [shift_x(normed, -m) for m in range(1, fsdp)]

    blocks = proj_weight.reshape(depth, 4, fsdp, pair, head_dim).transpose(2, 0, 1, 3, 4)
    mine = lax.dynamic_index_in_dim(blocks, core, axis=3, keepdims=False)
    eighth = out_weight.reshape(depth, fsdp, 2, cols // 2).transpose(1, 2, 0, 3)
    eighth = lax.dynamic_index_in_dim(eighth, core, axis=1, keepdims=False)
    sent = [blocks[:, :, 2].reshape(fsdp, depth, cols), eighth]
    sent = jnp.concatenate(sent + [mine[:, :, 0], mine[:, :, 1], mine[:, :, 3]], axis=-1)
    sent = jnp.broadcast_to(sent[None], (hist,) + sent.shape).reshape(hist * fsdp, depth, -1)
    weights = lax.all_to_all(sent, both, 0, 0).reshape(width, -1)
    def own_cache(member):
        at = (lax.div(member, pair), 0, f * cols + lax.rem(member, pair) * head_dim)
        size = (1, span, head_dim)
        return jnp.concatenate(
            [lax.dynamic_slice(hist_keys, at, size), lax.dynamic_slice(hist_values, at, size)]
        )

    caches = [own_cache(y)]
    caches += [shift_y(own_cache(lax.rem(y + k, members)), k) for k in range(1, members)]
    weights, caches, rows = lax.optimization_barrier((weights, caches, rows))
    w_other = swap_core(weights)

    work = 2 * fsdp * users * cand * width
    half = small_call(
        functools.partial(query_kernel, scale=0.5 / head_dim**0.5),
        "query",
        like(members, fsdp, cand, head_dim),
        place,
        *rows,
        weights,
        scalars=1,
        blocks={-1: (cols, 0)},
        flops=work * cols,
    )
    sent = half.reshape(members, fsdp * cand, head_dim)
    queries = lax.all_to_all(sent, "hist", 0, 0, axis_index_groups=along_y)
    queries = queries.reshape(members * fsdp * cand, head_dim)

    queries = [queries] + [shift_z(queries, -m) for m in range(1, outer)]

    w_out = [w[:, cols : cols + cols // 2] for w in (weights, w_other)]
    w_out = jnp.concatenate(w_out, axis=-1)
    w_out = [w_out] + [shift_x(w_out, m) for m in range(1, fsdp)]

    sources = lax.rem(y + members - jnp.arange(members, dtype=jnp.int32), members)
    starts = (sources * outer + z) * span
    counts = jnp.clip(lengths[lax.div(y, pair)] - starts, 0, span).astype(jnp.int32)
    back = small_call(
        rest_kernel,
        "rest",
        [like(2, users, cand, cols)] * fsdp,
        place,
        *rows,
        half,
        weights,
        w_other,
        scalars=1,
        blocks={-2: (3 * head_dim, 1), -1: (3 * head_dim, 1)},
        flops=work * cols * 3,
    )
    split = queries[0].shape[0] // 2
    head, tail = queries[0][:split], queries[0][split:]
    own = [attend(head, caches, counts)]
    last = own[0]
    parts = []
    for m in [1, outer - 1] + list(range(2, outer - 1)):
        ready, last = lax.optimization_barrier((queries[m], last))
        if not parts:
            own[0] = last
        elif len(parts) == outer - 2:
            ready, w_out = lax.optimization_barrier((ready, w_out))
        last = attend(ready, caches, counts)
        parts.append(shift_z(last, m))
    tail, last = lax.optimization_barrier((tail, last))
    own.append(attend(tail, caches, counts))
    parts.append(jnp.concatenate(own))
    back = [back[0]] + [shift_x(back[k], k) for k in range(1, fsdp)]

    total = sum(p.astype(jnp.float32) for p in parts).astype(jnp.bfloat16)
    total, back = lax.optimization_barrier((total, back))
    total = total.reshape(members * fsdp, cand, head_dim)
    total = lax.all_to_all(total, both, 0, 0, axis_index_groups=across)
    wide = pltpu.VMEM((users, cand, width), jnp.float32)
    return small_call(
        finish_kernel,
        "finish",
        like(users, cand, width),
        place,
        candidates,
        total,
        *back,
        *w_out,
        scalars=1,
        scratch=[wide, wide],
        flops=2 * users * cand * width * width,
    )


def solution(mesh):
    placed = (
        P("user", ("hist", "fsdp"), None),
        P("user", "hist", None),
        P("user", "hist", None),
        P("user"),
        P(("hist", "fsdp"), None),
        P(("hist", "fsdp"), None),
    )
    sizes = (mesh.shape["user"], mesh.shape["hist"], mesh.shape["fsdp"])
    return jax.shard_map(
        functools.partial(local, sizes),
        mesh=mesh,
        in_specs=placed,
        out_specs=P("user", ("hist", "fsdp"), None),
        check_vma=False,
    )
```

```python
import functools

import jax
import jax.numpy as jnp
from jax import lax
from jax.experimental import pallas as pl
from jax.experimental.pallas import tpu as pltpu
from jax.sharding import PartitionSpec as P

HEADS = 8


IN_SMEM = pl.BlockSpec(memory_space=pltpu.SMEM)


def layer_norm(x):
    mean = jnp.mean(x, axis=-1, keepdims=True)
    centered = x - mean
    var = jnp.mean(centered * centered, axis=-1, keepdims=True)
    return centered * lax.rsqrt(var + 1e-06)


def small_call(kernel, name, out_shape, *args, scalars=0, scratch=(), blocks=None, flops=0):
    specs = [IN_SMEM] * scalars
    for n, a in enumerate(args[scalars:]):
        width, at = (blocks or {}).get(n + scalars - len(args), (a.shape[-1], 0))
        zeros = (0,) * (a.ndim - 1)
        specs.append(pl.BlockSpec(a.shape[:-1] + (width,), lambda i, z=zeros, c=at: z + (c,)))
    return pl.pallas_call(
        kernel,
        grid=(1,),
        in_specs=specs,
        out_specs=jax.tree.map(
            lambda o: pl.BlockSpec(o.shape, lambda i, n=len(o.shape): (0,) * n), out_shape
        ),
        out_shape=out_shape,
        scratch_shapes=scratch,
        compiler_params=pltpu.CompilerParams(vmem_limit_bytes=60 * 1024 * 1024),
        cost_estimate=pl.CostEstimate(flops=flops, bytes_accessed=1 << 20, transcendentals=0),
        name=name,
    )(*args)


def normalise_kernel(x_ref, o_ref):
    for u in range(x_ref.shape[0]):
        o_ref[u] = layer_norm(x_ref[u].astype(jnp.float32)).astype(o_ref.dtype)


def query_kernel(place, *refs, scale):
    *rows, w_ref, o_ref = refs
    fsdp = len(rows)
    members, _, cand, head_dim = o_ref.shape
    pair = members // rows[0].shape[0]
    w = w_ref[...]
    for m, row in enumerate(rows):
        at = lax.rem(place[0] + m, fsdp)
        users, _, width = row.shape
        flat = row[...].reshape(users * cand, width)
        out = jax.nn.silu(jnp.dot(flat, w, preferred_element_type=jnp.float32))
        out = (out * scale).astype(jnp.bfloat16)
        for u in range(users):
            for e in range(pair):
                o_ref[u * pair + e, at] = out[
                    u * cand : (u + 1) * cand, e * head_dim : (e + 1) * head_dim
                ]


def rest_kernel(place, *refs):
    fsdp = (len(refs) - 3) // 2
    rows, (q_ref, mine, other), outs = refs[:fsdp], refs[fsdp : fsdp + 3], refs[fsdp + 3 :]
    members, _, cand, head_dim = q_ref.shape
    users = rows[0].shape[0]
    pair = members // users
    for turn, w_ref in enumerate((mine, other)):
        head = lax.rem(place[1] + turn, 2)
        here = pl.ds(pl.multiple_of(head * head_dim, head_dim), head_dim)
        w = w_ref[...]
        for m in range(fsdp):
            at = lax.rem(place[0] + m, fsdp)
            flat = rows[m][...].reshape(users * cand, rows[m].shape[-1])
            both = jax.nn.silu(jnp.dot(flat, w, preferred_element_type=jnp.float32))
            for u in range(users):
                out = both[u * cand : (u + 1) * cand].astype(jnp.bfloat16)
                gate = out[:, :head_dim]
                value = out[:, head_dim : 2 * head_dim].astype(jnp.float32)
                key = out[:, 2 * head_dim :].astype(jnp.float32)
                half = q_ref[u * pair + head, at].astype(jnp.float32)
                score = 2.0 * jnp.sum(half * key, axis=-1, keepdims=True)
                outs[m][0, u, :, here] = (jax.nn.silu(score) * value).astype(jnp.bfloat16)
                outs[m][1, u, :, here] = gate


def finish_kernel(place, x_ref, t_ref, *refs):
    fsdp = (len(refs) - 3) // 2
    backs, weights, (o_ref, total, gate) = refs[:fsdp], refs[fsdp:-3], refs[-3:]
    users, cand, width = x_ref.shape
    pair = t_ref.shape[0] // users // fsdp
    head_dim = t_ref.shape[-1]
    cols = width // fsdp
    for u in range(users):
        for e in range(pair):
            for c in range(fsdp):
                lo = c * cols + e * head_dim
                total[u, :, lo : lo + head_dim] = t_ref[(u * pair + e) * fsdp + c].astype(
                    jnp.float32
                )
    for m, back in enumerate(backs):
        lo = pl.multiple_of(lax.rem(place[0] + fsdp - m, fsdp) * cols, cols)
        for u in range(users):
            total[u, :, pl.ds(lo, cols)] += back[0, u].astype(jnp.float32)
            gate[u, :, pl.ds(lo, cols)] = back[1, u].astype(jnp.float32)
    part = cols // 2
    mixed = [(layer_norm(total[u]) * gate[u]).astype(jnp.bfloat16) for u in range(users)]
    mixed = jnp.concatenate(mixed)
    for m, w_ref in enumerate(weights):
        out = jnp.dot(mixed, w_ref[...], preferred_element_type=jnp.float32)
        for turn in range(2):
            lo = lax.rem(place[0] + fsdp - m, fsdp) * cols
            lo = pl.multiple_of(lo + lax.rem(place[1] + turn, 2) * part, part)
            for u in range(users):
                here = out[u * cand : (u + 1) * cand, turn * part : (turn + 1) * part]
                here += x_ref[u, :, pl.ds(lo, part)].astype(jnp.float32)
                o_ref[u, :, pl.ds(lo, part)] = here.astype(o_ref.dtype)


def attend_kernel(counts, q_ref, *refs, step):
    *caches, o_ref, v_ref = refs
    span = caches[0].shape[1]

    slot = lax.broadcasted_iota(jnp.int32, (span, v_ref.shape[1]), 0)
    for s, cache in enumerate(caches):
        vals = jnp.where(slot < counts[s], cache[1].astype(jnp.float32), 0.0)
        v_ref[pl.ds(s * span, span), :] = vals.astype(jnp.bfloat16)

    q = q_ref[...]
    total = None
    for s, cache in enumerate(caches):
        for j in range(0, span, step):
            half = lax.dot_general(
                q,
                cache[0, pl.ds(j, step), :],
                (((1,), (1,)), ((), ())),
                preferred_element_type=jnp.float32,
            )
            weights = (half + half * jnp.tanh(half)).astype(jnp.bfloat16)
            term = jnp.dot(
                weights,
                v_ref[pl.ds(s * span + j, step), :],
                preferred_element_type=jnp.float32,
            )
            total = term if total is None else total + term
    o_ref[...] = total.astype(o_ref.dtype)


def attend(half_queries, caches, counts, step=256):
    rows, head_dim = half_queries.shape
    _, span, _ = caches[0].shape
    slots = len(caches) * span
    in_vmem = pl.BlockSpec(memory_space=pltpu.VMEM)
    return pl.pallas_call(
        functools.partial(attend_kernel, step=step),
        in_specs=[pl.BlockSpec(memory_space=pltpu.SMEM)] + [in_vmem] * (1 + len(caches)),
        out_specs=in_vmem,
        scratch_shapes=[pltpu.VMEM((slots, head_dim), jnp.bfloat16)],
        out_shape=jax.ShapeDtypeStruct((rows, head_dim), jnp.bfloat16),
        compiler_params=pltpu.CompilerParams(vmem_limit_bytes=32 * 1024 * 1024),
        cost_estimate=pl.CostEstimate(
            flops=8 * rows * slots * head_dim,
            bytes_accessed=4 * rows * head_dim + 4 * slots * head_dim,
            transcendentals=rows * slots,
        ),
        name="attend",
    )(counts, half_queries, *caches)


def local(sizes, candidates, hist_keys, hist_values, lengths, proj_weight, out_weight):
    user_axis, hist, fsdp = sizes
    users, cand, width = candidates.shape
    head_dim = width // HEADS
    span = hist_keys.shape[1]
    both = ("hist", "fsdp")
    cols = width // fsdp
    pair = cols // head_dim
    members = users * pair
    outer = hist // members
    f = lax.axis_index("fsdp")
    h = lax.axis_index("hist")
    y, z = lax.div(h, outer), lax.rem(h, outer)
    core = lax.rem(lax.axis_index("user"), 2)
    depth = proj_weight.shape[0]
    along_y = [[a * outer + b for a in range(members)] for b in range(outer)]
    across = [
        [(a * outer + b) * fsdp + c for a in range(members) for c in range(fsdp)]
        for b in range(outer)
    ]

    def shift_x(a, k):
        return lax.ppermute(a, "fsdp", [(i, (i + k) % fsdp) for i in range(fsdp)])

    def shift_y(a, k):
        to = [(i, (i + k * outer) % hist) for i in range(hist)]
        return lax.ppermute(a, "hist", to)

    def shift_z(a, k):
        to = [(i, i - i % outer + (i + k) % outer) for i in range(hist)]
        return lax.ppermute(a, "hist", to)

    def swap_core(a):
        return lax.ppermute(a, "user", [(i, i ^ 1) for i in range(user_axis)])

    place = jnp.stack([f, core]).astype(jnp.int32)

    def like(*shape):
        return jax.ShapeDtypeStruct(shape, jnp.bfloat16)

    normed = small_call(
        normalise_kernel, "normalise", like(*candidates.shape), candidates, flops=1 << 20
    )
    rows = [normed] + [shift_x(normed, -m) for m in range(1, fsdp)]

    blocks = proj_weight.reshape(depth, 4, fsdp, pair, head_dim).transpose(2, 0, 1, 3, 4)
    mine = lax.dynamic_index_in_dim(blocks, core, axis=3, keepdims=False)
    eighth = out_weight.reshape(depth, fsdp, 2, cols // 2).transpose(1, 2, 0, 3)
    eighth = lax.dynamic_index_in_dim(eighth, core, axis=1, keepdims=False)
    sent = [blocks[:, :, 2].reshape(fsdp, depth, cols), eighth]
    sent = jnp.concatenate(sent + [mine[:, :, 0], mine[:, :, 1], mine[:, :, 3]], axis=-1)
    sent = jnp.broadcast_to(sent[None], (hist,) + sent.shape).reshape(hist * fsdp, depth, -1)
    weights = lax.all_to_all(sent, both, 0, 0).reshape(width, -1)
    def own_cache(member):
        at = (lax.div(member, pair), 0, f * cols + lax.rem(member, pair) * head_dim)
        size = (1, span, head_dim)
        return jnp.concatenate(
            [lax.dynamic_slice(hist_keys, at, size), lax.dynamic_slice(hist_values, at, size)]
        )

    caches = [own_cache(y)]
    caches += [shift_y(own_cache(lax.rem(y + k, members)), k) for k in range(1, members)]
    weights, caches, rows = lax.optimization_barrier((weights, caches, rows))
    w_other = swap_core(weights)

    work = 2 * fsdp * users * cand * width
    half = small_call(
        functools.partial(query_kernel, scale=0.5 / head_dim**0.5),
        "query",
        like(members, fsdp, cand, head_dim),
        place,
        *rows,
        weights,
        scalars=1,
        blocks={-1: (cols, 0)},
        flops=work * cols,
    )
    sent = half.reshape(members, fsdp * cand, head_dim)
    queries = lax.all_to_all(sent, "hist", 0, 0, axis_index_groups=along_y)
    queries = queries.reshape(members * fsdp * cand, head_dim)

    queries = [queries] + [shift_z(queries, -m) for m in range(1, outer)]

    w_out = [w[:, cols : cols + cols // 2] for w in (weights, w_other)]
    w_out = jnp.concatenate(w_out, axis=-1)
    w_out = [w_out] + [shift_x(w_out, m) for m in range(1, fsdp)]

    sources = lax.rem(y + members - jnp.arange(members, dtype=jnp.int32), members)
    starts = (sources * outer + z) * span
    counts = jnp.clip(lengths[lax.div(y, pair)] - starts, 0, span).astype(jnp.int32)
    back = small_call(
        rest_kernel,
        "rest",
        [like(2, users, cand, cols)] * fsdp,
        place,
        *rows,
        half,
        weights,
        w_other,
        scalars=1,
        blocks={-2: (3 * head_dim, 1), -1: (3 * head_dim, 1)},
        flops=work * cols * 3,
    )
    last = attend(queries[0], caches, counts)
    parts = [last]
    for m in [1, outer - 1] + list(range(2, outer - 1)):
        ready, last = lax.optimization_barrier((queries[m], last))
        if len(parts) == 1:
            parts[0] = last
            ready, back = lax.optimization_barrier((ready, back))
        elif len(parts) == outer - 1:
            ready, w_out = lax.optimization_barrier((ready, w_out))
        last = attend(ready, caches, counts)
        parts.append(shift_z(last, m))
    back = [back[0]] + [shift_x(back[k], k) for k in range(1, fsdp)]

    total = sum(p.astype(jnp.float32) for p in parts).astype(jnp.bfloat16)
    total, back = lax.optimization_barrier((total, back))
    total = total.reshape(members * fsdp, cand, head_dim)
    total = lax.all_to_all(total, both, 0, 0, axis_index_groups=across)
    wide = pltpu.VMEM((users, cand, width), jnp.float32)
    return small_call(
        finish_kernel,
        "finish",
        like(users, cand, width),
        place,
        candidates,
        total,
        *back,
        *w_out,
        scalars=1,
        scratch=[wide, wide],
        flops=2 * users * cand * width * width,
    )


def solution(mesh):
    placed = (
        P("user", ("hist", "fsdp"), None),
        P("user", "hist", None),
        P("user", "hist", None),
        P("user"),
        P(("hist", "fsdp"), None),
        P(("hist", "fsdp"), None),
    )
    sizes = (mesh.shape["user"], mesh.shape["hist"], mesh.shape["fsdp"])
    return jax.shard_map(
        functools.partial(local, sizes),
        mesh=mesh,
        in_specs=placed,
        out_specs=P("user", ("hist", "fsdp"), None),
        check_vma=False,
    )
```
